32 devices in a mesh: row: 4 (over y, x), col: 8 (over z, core).
Axes of the slice: x: 2, y: 2, z: 4, core: 2. Of those that a mesh axis runs over, the one named last changes fastest.
Arguments:
- tile_values: bfloat16 [384, 2048, 256], P('row', 'col'), may hold values from -0.0546875 to 0.0546875
- tile_rows: int32 [384, 8], P('row', 'col'), may hold values from 0 to 15
- tile_cols: int32 [384, 8], P('row', 'col'), may hold values from 0 to 15
- objective: float32 [32768], P('col'), may hold values from -13 to 13
- demand: float32 [16384, 128], P(('row', 'col')), may hold values from -40 to 40
- lower_bound: float32 [32768], P('col'), may hold values from -1 to 0
- bound_span: float32 [32768], P('col'), may hold values from 0.2 to 2
- bound_types: int32 [32768], P('col'), may hold values from 0 to 2
- primal_start: float32 [32768, 128], P('col'), may hold values from -3 to 3
- dual_start: float32 [16384, 128], P(('row', 'col')), may hold values from -2 to 2
Outputs:
- primal: float32 [32768, 128], P('col')
- dual_final: float32 [16384, 128], P(('row', 'col'))
- primal_weight: float32 [128], replicated
The draws below stay inside these ranges and needn't reach their ends.
Inputs may be any that keep to these rules, and one draw needn't show every extreme that they name: `tile_rows`: tile row of a tile inside its device's 16 tile rows; every device holds exactly 96 tiles and positions may repeat. `tile_cols`: tile column of a tile inside its device's 16 tile columns. `bound_types`: 0: free, 1: lower bound only, 2: both bounds.
All inputs are finite; a program needn't handle non-finite values.
Results may differ from the reference program's by a relative error of at most 0.0015.
Values may be sent and summed in bfloat16 or wider, within the bound.
A program may use at most 128 MiB of HBM per device.

```python
import math
import jax
import jax.numpy as jnp
from jax import lax

TS = 256
S = 128
RT = 16
CT = 16
TPD = 96
ITERS = 2
NC = 16384
NV = 32768
N_ROW = 4
N_COL = 8


def draw_objective(key, part):
    key = jax.random.fold_in(key, 11)
    key_base, key_scale = jax.random.split(key)
    base = jnp.clip(jax.random.normal(key_base, (NV,), jnp.float32), -4.0, 4.0)
    rough = jax.random.uniform(key_scale, (NV,), jnp.float32)
    ramp = 1.0 + 2.0 * jnp.arange(NV, dtype=jnp.float32) / max(NV - 1, 1)
    return base * 10.0 ** (rough - 1.0) * ramp


def draw_demand(key, part):
    key = jax.random.fold_in(key, 23)
    key_base, key_rows, key_scen = jax.random.split(key, 3)
    base = jnp.clip(jax.random.normal(key_base, (NC, S), jnp.float32), -4.0, 4.0)
    rough = jax.random.uniform(key_rows, (NC, 1), jnp.float32)
    scenario = 10.0 ** jax.random.uniform(key_scen, (1, S), jnp.float32, -0.5, 0.5)
    ramp = 1.0 + 2.0 * jnp.arange(NC, dtype=jnp.float32)[:, None] / max(NC - 1, 1)
    return base * 10.0 ** (rough - 1.0) * ramp * scenario


def place_ends(result, stream_key, low, largest):
    shape = result.shape
    index_at = [jax.random.randint(jax.random.fold_in(stream_key, axis), (), 0, shape[axis]) for axis in range(len(shape))]
    result = result.at[tuple(index_at)].set(low)
    longest = shape.index(max(shape))
    index_at[longest] = (index_at[longest] + 1) % shape[longest]
    return result.at[tuple(index_at)].set(largest)


def level_of(own_key, dims, shards, low, high):
    loudness, own = 1.0, jax.random.fold_in(own_key, 6)
    for dim, shards_of in shards:
        heights = jnp.exp(jax.random.uniform(jax.random.fold_in(own, dim), (shards_of,), jnp.float32, low / len(shards), high / len(shards)))
        loudness = loudness * jnp.repeat(heights, dims[dim] // shards_of).reshape([-1 if axis == dim else 1 for axis in range(len(dims))])
    return loudness


def bell_draw(rng, extent, scale, bound, shards=(), held_as=jnp.bfloat16):
    values = jax.random.normal(rng, extent, jnp.float32) * scale
    if len(shards) > 0:
        values = level_of(rng, extent, shards, -0.22, 0.18) * values
    return jnp.clip(values, min=-bound, max=bound).astype(held_as)


def setup_inputs(seed: int = 0) -> dict:
    splits = jax.random.split(jax.random.key(seed), 11)
    return {
        "tile_values": bell_draw(splits[0], (N_ROW * TPD, N_COL * TS, TS), (TPD * TS * N_COL // RT) ** -0.5, 0.0546875, ((0, 4), (1, 8))),
        "tile_rows": place_ends(jax.random.randint(splits[1], (N_ROW * TPD, N_COL), 0, RT), jax.random.fold_in(splits[1], 1), 0, RT - 1).astype(jnp.int32),
        "tile_cols": place_ends(jax.random.randint(splits[2], (N_ROW * TPD, N_COL), 0, CT), jax.random.fold_in(splits[2], 1), 0, CT - 1).astype(jnp.int32),
        "objective": draw_objective(jax.random.fold_in(splits[10], 71), 0),
        "demand": draw_demand(jax.random.fold_in(splits[10], 71), 0),
        "lower_bound": jnp.clip(-1.0 + 1.0 * jax.random.uniform(splits[5], (NV,), jnp.float32) ** level_of(splits[5], (NV,), ((0, 8),), -0.2, 0.2), -1.0, 0.0),
        "bound_span": jnp.clip(jnp.exp(math.log(2.0) - 2.3025851 * jax.random.uniform(splits[6], (NV,), jnp.float32) ** level_of(splits[6], (NV,), ((0, 8),), -0.2, 0.2)), 0.2, 2.0),
        "bound_types": place_ends(jax.random.randint(splits[7], (NV,), 0, 3), jax.random.fold_in(splits[7], 1), 0, 2).astype(jnp.int32),
        "primal_start": bell_draw(splits[8], (NV, S), 0.5, 3.0, ((0, 8),), jnp.float32),
        "dual_start": bell_draw(splits[9], (NC, S), 0.3, 2.0, ((0, 32),), jnp.float32),
    }


eps_norm = 1e-06
step_scale = 0.4

def forward_block(tile_block, row_ids, col_ids, vector_block, count_rows, count_cols):
    tile_size = tile_block.shape[1]
    width = vector_block.shape[1]
    pieces = vector_block.reshape(count_cols, tile_size, width)[col_ids]
    products = jnp.einsum('tij,tjs->tis', tile_block.astype(jnp.float32), pieces.astype(jnp.float32), precision=lax.Precision.HIGHEST)
    selector = (jnp.arange(count_rows, dtype=jnp.int32)[:, None] == row_ids[None, :]).astype(jnp.float32)
    summed = jnp.einsum('rt,tis->ris', selector, products, precision=lax.Precision.HIGHEST)
    return summed.reshape(count_rows * tile_size, width)

def transpose_block(tile_block, row_ids, col_ids, vector_block, count_rows, count_cols):
    tile_size = tile_block.shape[1]
    width = vector_block.shape[1]
    pieces = vector_block.reshape(count_rows, tile_size, width)[row_ids]
    products = jnp.einsum('tij,tis->tjs', tile_block.astype(jnp.float32), pieces.astype(jnp.float32), precision=lax.Precision.HIGHEST)
    selector = (jnp.arange(count_cols, dtype=jnp.int32)[:, None] == col_ids[None, :]).astype(jnp.float32)
    summed = jnp.einsum('ct,tjs->cjs', selector, products, precision=lax.Precision.HIGHEST)
    return summed.reshape(count_cols * tile_size, width)

def project(value, lower_bound, bound_span, bound_types):
    low_edge = lower_bound[:, None]
    high_edge = low_edge + bound_span[:, None]
    bound_kind = bound_types[:, None]
    raised = jnp.maximum(value, low_edge)
    boxed = jnp.minimum(raised, high_edge)
    return jnp.where(bound_kind == 0, value, jnp.where(bound_kind == 1, raised, boxed))

def reference(tile_values, tile_rows, tile_cols, objective, demand, lower_bound, bound_span, bound_types, primal_start, dual_start):
    blocked = tile_values.reshape(N_ROW, TPD, N_COL, TS, TS)
    rows_grid = tile_rows.reshape(N_ROW, TPD, N_COL)
    cols_grid = tile_cols.reshape(N_ROW, TPD, N_COL)
    device_ids = jnp.arange(N_ROW * N_COL, dtype=jnp.int32)

    def apply_forward(mixed):
        column_blocks = mixed.reshape(N_COL, CT * TS, S)

        def device_term(device):
            row_band = device // N_COL
            col_group = device % N_COL
            return forward_block(blocked[row_band, :, col_group], rows_grid[row_band, :, col_group], cols_grid[row_band, :, col_group], column_blocks[col_group], RT, CT)
        terms = lax.map(device_term, device_ids)
        return lax.optimization_barrier(jnp.sum(terms.reshape(N_ROW, N_COL, RT * TS, S), axis=1)).reshape(NC, S)

    def apply_transpose(dual_rows):
        row_blocks = dual_rows.reshape(N_ROW, RT * TS, S)

        def device_term(device):
            row_band = device // N_COL
            col_group = device % N_COL
            return transpose_block(blocked[row_band, :, col_group], rows_grid[row_band, :, col_group], cols_grid[row_band, :, col_group], row_blocks[row_band], RT, CT)
        terms = lax.map(device_term, device_ids)
        return lax.optimization_barrier(jnp.sum(terms.reshape(N_ROW, N_COL, CT * TS, S), axis=0)).reshape(NV, S)
    cost_sq = jnp.sum(objective * objective)
    demand_sq = lax.optimization_barrier(jnp.sum(demand * demand, axis=0))
    weight = jnp.sqrt(cost_sq + eps_norm) / jnp.sqrt(demand_sq + eps_norm)
    primal = primal_start
    dual = dual_start
    for iteration in range(ITERS):
        step_primal = step_scale / weight
        step_dual = step_scale * weight
        pulled = apply_transpose(dual.astype(jnp.bfloat16))
        primal_next = project(primal - step_primal[None, :] * (objective[:, None] - pulled), lower_bound, bound_span, bound_types)
        moved = primal_next - primal
        primal_sq = lax.optimization_barrier(jnp.sum(moved * moved, axis=0))
        mixed = (2.0 * primal_next - primal).astype(jnp.bfloat16)
        pushed = apply_forward(mixed)
        change = step_dual[None, :] * (demand - pushed)
        dual = dual + change
        dual_sq = lax.optimization_barrier(jnp.sum(change * change, axis=0))
        weight = jnp.sqrt(weight * jnp.sqrt((dual_sq + eps_norm) / (primal_sq + eps_norm)))
        primal = primal_next
    return (primal, dual, weight)
```

```python
import functools
import jax
import jax.numpy as jnp
from jax import lax
from jax.experimental import pallas as pl
from jax.experimental.pallas import tpu as pltpu
from jax.sharding import PartitionSpec as P

ITERS = 2
CORES = 2

eps_norm = 1e-06
step_scale = 0.4
MESH = pl.DeviceIdType.MESH


def schedule(keys, others, count):
    total = keys.shape[0]
    order = jnp.arange(total, dtype=jnp.int32)
    ahead = (keys[None, :] < keys[:, None]) | (
        (keys[None, :] == keys[:, None]) & (order[None, :] < order[:, None])
    )
    rank = jnp.sum(ahead.astype(jnp.int32), axis=1)
    here = rank[None, :] == order[:, None]
    perm = jnp.sum(jnp.where(here, order[None, :], 0), axis=1)
    other = jnp.sum(jnp.where(here, others[None, :], 0), axis=1)
    first = here & ~jnp.any(
        (keys[None, :] == keys[:, None]) & (order[None, :] < order[:, None]), axis=1
    )[None, :]
    keep = 1 - jnp.sum(first.astype(jnp.int32), axis=1)
    ids = jnp.arange(count, dtype=jnp.int32)
    cnt = jnp.sum((keys[None, :] == ids[:, None]).astype(jnp.int32), axis=1)
    upto = jnp.sum((keys[None, :] <= ids[:, None]).astype(jnp.int32), axis=1)
    return jnp.stack([perm, other, keep]), jnp.stack([jnp.maximum(upto - 1, 0), cnt])


def kernel(
    n_row, n_col,
    plan_r, plan_c, ends_r, ends_c, tiles_any, params, demand, primal_any, dual_start,
    primal_out, dual_out, weight_out,
    tiles, primal, dual_rows, dual_t, run, pull_out, pull_own, pull_in, mixed,
    pair_out, pair_in, push_out, push_own, push_in, norm_row, norm_col,
    load_sem, gather_send, gather_recv, pass_send, pull_send, pull_recv,
    mix_send, mix_recv, final_send, final_recv, pair_send, pair_recv,
    push_send, push_recv, nrow_send, nrow_recv, ncol_send, ncol_recv,
):
    i, j = lax.axis_index("row"), lax.axis_index("col")
    n_chip = n_col // CORES
    chip, core = lax.div(j, CORES), lax.rem(j, CORES)
    other_core = 1 - core
    partner = (i, chip * CORES + other_core)
    total, size = tiles.shape[0], tiles.shape[1]
    share = demand.shape[0]
    quarter = primal.shape[0]
    blocks_c = n_row * quarter
    blocks_r = n_col * share
    width = demand.shape[2]
    half = size // 2
    sends = []

    def remote(src, dst, send_sem, recv_sem, device):
        return pltpu.make_async_remote_copy(
            src_ref=src, dst_ref=dst, send_sem=send_sem, recv_sem=recv_sem,
            device_id=device, device_id_type=MESH,
        )

    def send(*args):
        copy = remote(*args)
        copy.start()
        sends.append(copy)

    row_peer = [lax.rem(i + d, n_row) for d in range(n_row)]
    col_peer = [lax.rem(j + d, n_col) for d in range(n_col)]
    chip_peer = [lax.rem(chip + d, n_chip) for d in range(n_chip)]

    load_tiles = pltpu.make_async_copy(tiles_any, tiles, load_sem.at[0])
    load_tiles.start()
    load_primal = pltpu.make_async_copy(
        primal_any.at[pl.ds(i * quarter, quarter)], primal, load_sem.at[1]
    )
    load_primal.start()

    barrier = pltpu.get_barrier_semaphore()
    for d in range(1, n_row):
        pl.semaphore_signal(barrier, inc=1, device_id=(row_peer[d], j), device_id_type=MESH)
    for d in range(1, n_col):
        pl.semaphore_signal(barrier, inc=1, device_id=(i, col_peer[d]), device_id_type=MESH)
    pl.semaphore_wait(barrier, n_row + n_col - 2)

    def share_of(t, owner):
        return dual_rows.at[pl.ds(t * blocks_r + owner * share, share)]

    def gather_start(t):
        for d in range(1, n_chip):
            send(share_of(t, j), share_of(t, j), gather_send.at[t, d], gather_recv.at[t, j],
                 (i, chip_peer[d] * CORES + core))
        send(share_of(t, j), share_of(t, j), pass_send.at[t, 0], gather_recv.at[t, j], partner)

    def gather_finish(t):
        for d in range(1, n_chip):
            owner = chip_peer[n_chip - d] * CORES + core
            remote(share_of(t, owner), share_of(t, owner), gather_send.at[t, d],
                   gather_recv.at[t, owner], partner).wait_recv()
            send(share_of(t, owner), share_of(t, owner), pass_send.at[t, d],
                 gather_recv.at[t, owner], partner)
        for d in range(n_chip):
            owner = chip_peer[d] * CORES + other_core
            remote(share_of(t, owner), share_of(t, owner), pass_send.at[t, d],
                   gather_recv.at[t, owner], partner).wait_recv()

    def norm_start(t, first, second):
        norm_row[t * n_row + i] = jnp.concatenate(
            [first, second, jnp.zeros((6, width), jnp.float32)], axis=0
        )
        for d in range(1, n_row):
            slot = norm_row.at[t * n_row + i]
            send(slot, slot, nrow_send.at[t, d], nrow_recv.at[t, i], (row_peer[d], j))

    def norm_middle(t):
        for d in range(1, n_row):
            slot = norm_row.at[t * n_row + row_peer[d]]
            remote(slot, slot, nrow_send.at[t, d], nrow_recv.at[t, row_peer[d]],
                   (row_peer[d], j)).wait_recv()
        added = norm_row[t * n_row]
        for k in range(1, n_row):
            added = added + norm_row[t * n_row + k]
        norm_col[t * n_col + j] = added
        for d in range(1, n_col):
            slot = norm_col.at[t * n_col + j]
            send(slot, slot, ncol_send.at[t, d], ncol_recv.at[t, j], (i, col_peer[d]))

    def norm_finish(t):
        for d in range(1, n_col):
            slot = norm_col.at[t * n_col + col_peer[d]]
            remote(slot, slot, ncol_send.at[t, d], ncol_recv.at[t, col_peer[d]],
                   (i, col_peer[d])).wait_recv()
        added = norm_col[t * n_col]
        for k in range(1, n_col):
            added = added + norm_col[t * n_col + k]
        return added[0:1, :], added[1:2, :]

    zero_row = jnp.zeros((1, width), jnp.float32)

    def start_block(b, carry):
        value = dual_start[b]
        dual_out[b] = value
        dual_rows[j * share + b] = value.astype(jnp.bfloat16)
        wanted = demand[b]
        return carry + jnp.sum(wanted * wanted, axis=0, keepdims=True)

    demand_sq = lax.fori_loop(0, share, start_block, zero_row)
    gather_start(0)
    cost = params[:, 0:1]
    cost_sq = jnp.sum(cost * cost, axis=0, keepdims=True)
    norm_start(0, demand_sq, jnp.broadcast_to(cost_sq, (1, width)))
    norm_middle(0)
    weight = None
    load_primal.wait()
    load_tiles.wait()

    for t in range(ITERS):
        gather_finish(t)
        if t > 0:
            norm_middle(t)

        def turn(b, carry):
            dual_t[b] = dual_rows[t * blocks_r + b].astype(jnp.float32).T.astype(jnp.bfloat16)
            return carry

        lax.fori_loop(0, blocks_r, turn, 0)

        def pull_tile(n, before):
            added = jnp.dot(dual_t[plan_c[1, n]], tiles[plan_c[0, n]],
                            preferred_element_type=jnp.float32)
            added = added + jnp.where(plan_c[2, n] == 1, before, 0.0)
            run[n, 0:half, :] = added[:, 0:half]
            run[n, half:size, :] = added[:, half:size]
            return added

        lax.fori_loop(0, total, pull_tile, jnp.zeros((width, size), jnp.float32), unroll=4)

        def pulled_block(block, row):
            last = ends_c[0, block]
            held = ends_c[1, block] > 0
            return jnp.where(held, run[last, row:row + half, :], 0.0).T

        for d in range(1, n_row):
            dest = row_peer[d]

            def pack_pull(b, carry):
                at = dest * quarter + b
                for row in (0, half):
                    pull_out[t * blocks_c + at, row:row + half, :] = pulled_block(at, row).astype(
                        jnp.bfloat16)
                return carry

            lax.fori_loop(0, quarter, pack_pull, 0)
            send(pull_out.at[pl.ds(t * blocks_c + dest * quarter, quarter)],
                 pull_in.at[pl.ds(t * blocks_c + i * quarter, quarter)],
                 pull_send.at[t, d], pull_recv.at[t, i], (dest, j))

        def keep_pull(b, carry):
            for row in (0, half):
                pull_own[b, row:row + half, :] = pulled_block(i * quarter + b, row)
            return carry

        lax.fori_loop(0, quarter, keep_pull, 0)

        if t == 0:
            demand_all, cost_all = norm_finish(0)
            weight = jnp.sqrt(cost_all + eps_norm) / jnp.sqrt(demand_all + eps_norm)
        else:
            dual_all, primal_all = norm_finish(t)
            weight = jnp.sqrt(weight * jnp.sqrt((dual_all + eps_norm) / (primal_all + eps_norm)))
        step_primal = step_scale / weight
        step_dual = step_scale * weight

        for d in range(1, n_row):
            origin = row_peer[n_row - d]
            slot = pull_in.at[pl.ds(t * blocks_c + origin * quarter, quarter)]
            remote(slot, slot, pull_send.at[t, d], pull_recv.at[t, origin],
                   (origin, j)).wait_recv()

        def update_primal(b, carry):
            pulled = pull_own[b]
            for d in range(1, n_row):
                pulled = pulled + pull_in[
                    t * blocks_c + row_peer[d] * quarter + b].astype(jnp.float32)
            rows = pl.ds(pl.multiple_of(b * size, size), size)
            old = primal[b]
            value = old - step_primal * (params[rows, 0:1] - pulled)
            new = jnp.minimum(jnp.maximum(value, params[rows, 1:2]), params[rows, 2:3])
            moved = new - old
            mixed[t * blocks_c + i * quarter + b] = (2.0 * new - old).astype(jnp.bfloat16)
            if t == ITERS - 1:
                primal_out[i * quarter + b] = new
            else:
                primal[b] = new
            return carry + jnp.sum(moved * moved, axis=0, keepdims=True)

        primal_sq = lax.fori_loop(0, quarter, update_primal, zero_row)

        mine = mixed.at[pl.ds(t * blocks_c + i * quarter, quarter)]
        for d in range(1, n_row):
            send(mine, mine, mix_send.at[t, d], mix_recv.at[t, i], (row_peer[d], j))
        for d in range(1, n_row):
            origin = row_peer[n_row - d]
            slot = mixed.at[pl.ds(t * blocks_c + origin * quarter, quarter)]
            remote(slot, slot, mix_send.at[t, d], mix_recv.at[t, origin],
                   (origin, j)).wait_recv()
        if t == ITERS - 1:
            mine = primal_out.at[pl.ds(i * quarter, quarter)]
            for d in range(1, n_row):
                send(mine, mine, final_send.at[d], final_recv.at[i], (row_peer[d], j))

        def push_tile(n, before):
            added = jnp.dot(tiles[plan_r[0, n]], mixed[t * blocks_c + plan_r[1, n]],
                            preferred_element_type=jnp.float32)
            added = added + jnp.where(plan_r[2, n] == 1, before, 0.0)
            run[n] = added
            return added

        lax.fori_loop(0, total, push_tile, jnp.zeros((size, width), jnp.float32), unroll=4)

        def pushed_block(block):
            return jnp.where(ends_r[1, block] > 0, run[ends_r[0, block]], 0.0)

        def part(ref, owner_chip):
            return ref.at[pl.ds((t * n_chip + owner_chip) * share, share)]

        order = [*range(1, n_chip), 0]
        for d in order:
            dest = chip_peer[d]

            def pack_pair(b, carry):
                pair_out[(t * n_chip + dest) * share + b] = pushed_block(
                    (dest * CORES + other_core) * share + b).astype(pair_out.dtype)
                return carry

            lax.fori_loop(0, share, pack_pair, 0)
            send(part(pair_out, dest), part(pair_in, dest), pair_send.at[t, d],
                 pair_recv.at[t, dest], partner)
        for d in order:
            dest = chip_peer[d]
            slot = part(pair_in, dest)
            remote(slot, slot, pair_send.at[t, d], pair_recv.at[t, dest], partner).wait_recv()

            def pack_push(b, carry):
                at = (t * n_chip + dest) * share + b
                value = pushed_block((dest * CORES + core) * share + b) + pair_in[at].astype(
                    jnp.float32)
                if d == 0:
                    push_own[b] = value
                else:
                    push_out[at] = value.astype(jnp.bfloat16)
                return carry

            lax.fori_loop(0, share, pack_push, 0)
            if d != 0:
                send(part(push_out, dest), part(push_in, chip), push_send.at[t, d],
                     push_recv.at[t, chip], (i, dest * CORES + core))
        for d in range(1, n_chip):
            origin = chip_peer[n_chip - d]
            slot = part(push_in, origin)
            remote(slot, slot, push_send.at[t, d], push_recv.at[t, origin],
                   (i, origin * CORES + core)).wait_recv()

        def update_dual(b, carry):
            pushed = push_own[b]
            for d in range(1, n_chip):
                pushed = pushed + push_in[
                    (t * n_chip + chip_peer[d]) * share + b].astype(jnp.float32)
            change = step_dual * (demand[b] - pushed)
            new = dual_out[b] + change
            dual_out[b] = new
            if t < ITERS - 1:
                dual_rows[(t + 1) * blocks_r + j * share + b] = new.astype(jnp.bfloat16)
            return carry + jnp.sum(change * change, axis=0, keepdims=True)

        dual_sq = lax.fori_loop(0, share, update_dual, zero_row)
        norm_start(t + 1, dual_sq, primal_sq)
        if t < ITERS - 1:
            gather_start(t + 1)

    norm_middle(ITERS)
    dual_all, primal_all = norm_finish(ITERS)
    weight = jnp.sqrt(weight * jnp.sqrt((dual_all + eps_norm) / (primal_all + eps_norm)))
    weight_out[...] = jnp.broadcast_to(weight, weight_out.shape)
    for d in range(1, n_row):
        origin = row_peer[n_row - d]
        slot = primal_out.at[pl.ds(origin * quarter, quarter)]
        remote(slot, slot, final_send.at[d], final_recv.at[origin], (origin, j)).wait_recv()
    for copy in sends:
        copy.wait_send()


def on_device(
    tile_values, tile_rows, tile_cols, objective, demand, lower_bound, bound_span, bound_types,
    primal_start, dual_start,
):
    n_row, n_col = lax.axis_size("row"), lax.axis_size("col")
    total, size = tile_values.shape[0], tile_values.shape[1]
    width = demand.shape[1]
    share = dual_start.shape[0] // size
    blocks_r = share * n_col
    blocks_c = primal_start.shape[0] // size
    quarter = blocks_c // n_row
    n_chip = n_col // CORES
    row_ids, col_ids = tile_rows.reshape(-1), tile_cols.reshape(-1)
    plan_r, ends_r = schedule(row_ids, col_ids, blocks_r)
    plan_c, ends_c = schedule(col_ids, row_ids, blocks_c)
    low = jnp.where(bound_types == 0, -jnp.inf, lower_bound)
    high = jnp.where(bound_types == 2, lower_bound + bound_span, jnp.inf)
    params = lax.dynamic_slice_in_dim(
        jnp.stack([objective, low, high, jnp.zeros_like(low)], axis=1),
        lax.axis_index("row") * quarter * size, quarter * size, 0,
    )
    f32, bf16 = jnp.float32, jnp.bfloat16
    vmem, smem = pl.BlockSpec(memory_space=pltpu.VMEM), pl.BlockSpec(memory_space=pltpu.SMEM)
    anywhere = pl.BlockSpec(memory_space=pl.ANY)
    dma = pltpu.SemaphoreType.DMA

    def held(count, dtype):
        return pltpu.VMEM((count, size, width), dtype)

    primal, dual, weight = pl.pallas_call(
        functools.partial(kernel, n_row, n_col),
        out_shape=(
            jax.ShapeDtypeStruct((blocks_c, size, width), f32),
            jax.ShapeDtypeStruct((share, size, width), f32),
            jax.ShapeDtypeStruct((8, width), f32),
        ),
        in_specs=[smem, smem, smem, smem, anywhere, vmem, vmem, anywhere, vmem],
        out_specs=(vmem, vmem, vmem),
        scratch_shapes=[
            pltpu.VMEM((total, size, size), bf16),
            held(quarter, f32),
            held(ITERS * blocks_r, bf16),
            pltpu.VMEM((blocks_r, width, size), bf16),
            held(total, f32),
            held(ITERS * blocks_c, bf16),
            held(quarter, f32),
            held(ITERS * blocks_c, bf16),
            held(ITERS * blocks_c, bf16),
            held(ITERS * n_chip * share, f32),
            held(ITERS * n_chip * share, f32),
            held(ITERS * n_chip * share, bf16),
            held(share, f32),
            held(ITERS * n_chip * share, bf16),
            pltpu.VMEM(((ITERS + 1) * n_row, 8, width), f32),
            pltpu.VMEM(((ITERS + 1) * n_col, 8, width), f32),
            dma((2,)),
            dma((ITERS, n_chip)), dma((ITERS, n_col)), dma((ITERS, n_chip)),
            dma((ITERS, n_row)), dma((ITERS, n_row)),
            dma((ITERS, n_row)), dma((ITERS, n_row)),
            dma((n_row,)), dma((n_row,)),
            dma((ITERS, n_chip)), dma((ITERS, n_chip)),
            dma((ITERS, n_chip)), dma((ITERS, n_chip)),
            dma((ITERS + 1, n_row)), dma((ITERS + 1, n_row)),
            dma((ITERS + 1, n_col)), dma((ITERS + 1, n_col)),
        ],
        compiler_params=pltpu.CompilerParams(
            collective_id=0, has_side_effects=True, vmem_limit_bytes=54 * 2**20
        ),
        cost_estimate=pl.CostEstimate(
            flops=4 * ITERS * total * size * size * width,
            bytes_accessed=2 * total * size * size, transcendentals=0,
        ),
    )(
        plan_r, plan_c, ends_r, ends_c, tile_values, params,
        demand.reshape(share, size, width),
        primal_start.reshape(blocks_c, size, width),
        dual_start.reshape(share, size, width),
    )
    return primal.reshape(primal_start.shape), dual.reshape(dual_start.shape), weight[0]


def solution(mesh):
    return jax.shard_map(
        on_device,
        mesh=mesh,
        in_specs=(
            P("row", "col", None),
            P("row", "col"),
            P("row", "col"),
            P("col"),
            P(("row", "col"), None),
            P("col"),
            P("col"),
            P("col"),
            P("col", None),
            P(("row", "col"), None),
        ),
        out_specs=(P("col", None), P(("row", "col"), None), P()),
        check_vma=False,
    )
```

```python
import functools
import jax
import jax.numpy as jnp
from jax import lax
from jax.experimental import pallas as pl
from jax.experimental.pallas import tpu as pltpu
from jax.sharding import PartitionSpec as P

ITERS = 2
CORES = 2
HALVES = 2
OTHER_BIT, KEEP_BIT, COUNT_BIT = 12, 24, 16

eps_norm = 1e-06
step_scale = 0.4
MESH = pl.DeviceIdType.MESH


def schedule(keys, others, count):
    total = keys.shape[1]
    order = jnp.arange(total, dtype=jnp.int32)
    same = (keys[:, None, :] == keys[:, :, None]) & (order[None, :] < order[:, None])[None]
    ahead = same | (keys[:, None, :] < keys[:, :, None])
    rank = jnp.sum(ahead.astype(jnp.int32), axis=2)
    keep = jnp.max(same.astype(jnp.int32), axis=2)
    code = order[None, :] + (others << OTHER_BIT) + (keep << KEEP_BIT)
    here = rank[:, None, :] == order[None, :, None]
    plan = jnp.sum(jnp.where(here, code[:, None, :], 0), axis=2)
    ids = jnp.arange(count, dtype=jnp.int32)[None, :, None]
    upto = (keys[:, None, :] <= ids).astype(jnp.int32)
    equal = (keys[:, None, :] == ids).astype(jnp.int32)
    return plan, jnp.sum(upto + (equal << COUNT_BIT), axis=2)


def kernel(
    n_row, n_col,
    plan, ends, tiles_any, params, demand, primal_any, dual_start,
    primal_out, dual_out, weight_out,
    tiles, primal_in, primal, wanted, dual, dual_rows, run, pull_out, pull_own, pull_in, mixed,
    pair_out, pair_in, push_out, push_own, push_in, final, norm_row, norm_col,
    load_sem, gather_send, gather_recv, pass_send, pull_send, pull_recv,
    mix_send, mix_recv, final_send, final_recv, pair_send, pair_recv,
    push_send, push_recv, nrow_send, nrow_recv, ncol_send, ncol_recv,
):
    i, j = lax.axis_index("row"), lax.axis_index("col")
    n_chip = n_col // CORES
    chip, core = lax.div(j, CORES), lax.rem(j, CORES)
    other_core = 1 - core
    partner = (i, chip * CORES + other_core)
    total, size = tiles.shape[0], tiles.shape[1]
    share, width = demand.shape[0], demand.shape[2]
    lanes = width // HALVES
    quarter = primal_in.shape[0]
    blocks_c = n_row * quarter
    blocks_r = n_col * share
    f32, bf16 = jnp.float32, jnp.bfloat16
    sends = []

    def remote(src, dst, send_sem, recv_sem, device):
        return pltpu.make_async_remote_copy(
            src_ref=src, dst_ref=dst, send_sem=send_sem, recv_sem=recv_sem,
            device_id=device, device_id_type=MESH,
        )

    def send(*args):
        copy = remote(*args)
        copy.start()
        sends.append(copy)

    row_peer = [lax.rem(i + d, n_row) for d in range(n_row)]
    col_peer = [lax.rem(j + d, n_col) for d in range(n_col)]
    chip_peer = [lax.rem(chip + d, n_chip) for d in range(n_chip)]

    load_tiles = pltpu.make_async_copy(tiles_any, tiles, load_sem.at[0])
    load_tiles.start()
    load_primal = pltpu.make_async_copy(
        primal_any.at[pl.ds(i * quarter, quarter)], primal_in, load_sem.at[1]
    )
    load_primal.start()

    barrier = pltpu.get_barrier_semaphore()
    for d in range(1, n_row):
        pl.semaphore_signal(barrier, inc=1, device_id=(row_peer[d], j), device_id_type=MESH)
    for d in range(1, n_col):
        pl.semaphore_signal(barrier, inc=1, device_id=(i, col_peer[d]), device_id_type=MESH)

    zero = jnp.zeros((lanes, 1), f32)

    def squares(value):
        return jnp.sum(value * value, axis=1, keepdims=True)

    def share_of(p, owner):
        return dual_rows[p].at[pl.ds(owner * share, share)]

    def gather_start(p):
        for d in range(1, n_chip):
            send(share_of(p, j), share_of(p, j), gather_send.at[p, d], gather_recv.at[p, j],
                 (i, chip_peer[d] * CORES + core))
        send(share_of(p, j), share_of(p, j), pass_send.at[p, 0], gather_recv.at[p, j], partner)

    def gather_finish(p):
        for d in range(1, n_chip):
            owner = chip_peer[n_chip - d] * CORES + core
            remote(share_of(p, owner), share_of(p, owner), gather_send.at[p, d],
                   gather_recv.at[p, owner], partner).wait_recv()
            send(share_of(p, owner), share_of(p, owner), pass_send.at[p, d],
                 gather_recv.at[p, owner], partner)
        for d in range(n_chip):
            owner = chip_peer[d] * CORES + other_core
            remote(share_of(p, owner), share_of(p, owner), pass_send.at[p, d],
                   gather_recv.at[p, owner], partner).wait_recv()

    def norm_start(p, first, second):
        lane = lax.broadcasted_iota(jnp.int32, (lanes, width), 1)
        laid = jnp.where(lane == 0, first, jnp.where(lane == 1, second, 0.0))
        square = jnp.concatenate([laid, jnp.zeros((width - lanes, width), f32)], axis=0)
        norm_row[p * n_row + i] = square.T[0:8, :]
        for d in range(1, n_row):
            slot = norm_row.at[p * n_row + i]
            send(slot, slot, nrow_send.at[p, d], nrow_recv.at[p, i], (row_peer[d], j))

    def norm_middle(p):
        for d in range(1, n_row):
            slot = norm_row.at[p * n_row + row_peer[d]]
            remote(slot, slot, nrow_send.at[p, d], nrow_recv.at[p, row_peer[d]],
                   (row_peer[d], j)).wait_recv()
        added = norm_row[p * n_row]
        for k in range(1, n_row):
            added = added + norm_row[p * n_row + k]
        norm_col[p * n_col + j] = added
        for d in range(1, n_col):
            slot = norm_col.at[p * n_col + j]
            send(slot, slot, ncol_send.at[p, d], ncol_recv.at[p, j], (i, col_peer[d]))

    def norm_finish(p):
        for d in range(1, n_col):
            slot = norm_col.at[p * n_col + col_peer[d]]
            remote(slot, slot, ncol_send.at[p, d], ncol_recv.at[p, col_peer[d]],
                   (i, col_peer[d])).wait_recv()
        added = norm_col[p * n_col]
        for k in range(1, n_col):
            added = added + norm_col[p * n_col + k]
        square = jnp.concatenate([added, jnp.zeros((width - 8, width), f32)], axis=0).T
        return square[0:lanes, 0:1], square[0:lanes, 1:2]

    weight = [None] * HALVES
    primal_sq = [None] * HALVES

    def begin(b, carry):
        rows = dual_start[b].T
        right = demand[b].T
        out = []
        for h in range(HALVES):
            part = rows[h * lanes:(h + 1) * lanes, :]
            dual[h * share + b] = part
            dual_rows[h][j * share + b] = part.astype(bf16)
            part = right[h * lanes:(h + 1) * lanes, :]
            wanted[h * share + b] = part
            out.append(carry[h] + squares(part))
        return tuple(out)

    demand_sq = lax.fori_loop(0, share, begin, (zero,) * HALVES)
    pl.semaphore_wait(barrier, n_row + n_col - 2)
    cost_sq = jnp.broadcast_to(squares(params[0:1, :]), (lanes, 1))
    for h in range(HALVES):
        gather_start(h)
        norm_start(h, demand_sq[h], cost_sq)
    load_primal.wait()

    def turn(b, carry):
        rows = primal_in[b].T
        for h in range(HALVES):
            primal[h * quarter + b] = rows[h * lanes:(h + 1) * lanes, :]
        return carry

    lax.fori_loop(0, quarter, turn, 0)
    load_tiles.wait()

    def multiply(which, source, dims):
        def one(n, before):
            code = plan[which, n]
            tile = code & ((1 << OTHER_BIT) - 1)
            other = (code >> OTHER_BIT) & ((1 << (KEEP_BIT - OTHER_BIT)) - 1)
            added = lax.dot_general(source[other], tiles[tile], (dims, ((), ())),
                                    preferred_element_type=f32)
            added = added + jnp.where((code >> KEEP_BIT) == 1, before, 0.0)
            run[n] = added
            return added

        lax.fori_loop(0, total, one, jnp.zeros((lanes, size), f32), unroll=8)

    def summed(which, block):
        code = ends[which, block]
        last = jnp.maximum((code & ((1 << COUNT_BIT) - 1)) - 1, 0)
        return jnp.where((code >> COUNT_BIT) > 0, run[last], 0.0)

    def pull(t, h):
        p = t * HALVES + h
        gather_finish(p)
        norm_middle(p)
        multiply(1, dual_rows[p], ((1,), (0,)))
        for d in range(1, n_row):
            dest = row_peer[d]

            def pack(b, carry):
                at = dest * quarter + b
                pull_out[p * blocks_c + at] = summed(1, at).astype(bf16)
                return carry

            lax.fori_loop(0, quarter, pack, 0)
            send(pull_out.at[pl.ds(p * blocks_c + dest * quarter, quarter)],
                 pull_in.at[pl.ds(p * blocks_c + i * quarter, quarter)],
                 pull_send.at[p, d], pull_recv.at[p, i], (dest, j))

        def own(b, carry):
            pull_own[h * quarter + b] = summed(1, i * quarter + b)
            return carry

        lax.fori_loop(0, quarter, own, 0)

    def new_weight(p, h):
        dual_all, primal_all = norm_finish(p)
        if p < HALVES:
            weight[h] = jnp.sqrt(primal_all + eps_norm) / jnp.sqrt(dual_all + eps_norm)
        else:
            weight[h] = jnp.sqrt(
                weight[h] * jnp.sqrt((dual_all + eps_norm) / (primal_all + eps_norm)))

    def update_primal(t, h):
        p = t * HALVES + h
        new_weight(p, h)
        step = step_scale / weight[h]
        for d in range(1, n_row):
            origin = row_peer[n_row - d]
            slot = pull_in.at[pl.ds(p * blocks_c + origin * quarter, quarter)]
            remote(slot, slot, pull_send.at[p, d], pull_recv.at[p, origin],
                   (origin, j)).wait_recv()

        def one(b, carry):
            pulled = pull_own[h * quarter + b]
            for d in range(1, n_row):
                pulled = pulled + pull_in[
                    p * blocks_c + row_peer[d] * quarter + b].astype(f32)
            at = pl.ds(pl.multiple_of(b * size, size), size)
            old = primal[h * quarter + b]
            value = old - step * (params[0:1, at] - pulled)
            new = jnp.minimum(jnp.maximum(value, params[1:2, at]), params[2:3, at])
            mixed[p][i * quarter + b] = (2.0 * new - old).astype(bf16)
            if t == ITERS - 1:
                final[h * blocks_c + i * quarter + b] = new
            else:
                primal[h * quarter + b] = new
            return carry + squares(new - old)

        primal_sq[h] = lax.fori_loop(0, quarter, one, zero)
        mine = mixed[p].at[pl.ds(i * quarter, quarter)]
        for d in range(1, n_row):
            send(mine, mine, mix_send.at[p, d], mix_recv.at[p, i], (row_peer[d], j))

    def send_final(h):
        mine = final.at[pl.ds(h * blocks_c + i * quarter, quarter)]
        for d in range(1, n_row):
            send(mine, mine, final_send.at[h, d], final_recv.at[h, i], (row_peer[d], j))

    def mixed_wait(p):
        for d in range(1, n_row):
            origin = row_peer[n_row - d]
            slot = mixed[p].at[pl.ds(origin * quarter, quarter)]
            remote(slot, slot, mix_send.at[p, d], mix_recv.at[p, origin],
                   (origin, j)).wait_recv()

    order = [*range(1, n_chip), 0]

    def push(t, h):
        p = t * HALVES + h
        mixed_wait(p)
        if t == ITERS - 1:
            send_final(h)
        multiply(0, mixed[p], ((1,), (1,)))

        def part(ref, owner_chip):
            return ref.at[pl.ds((p * n_chip + owner_chip) * share, share)]

        for d in order:
            dest = chip_peer[d]

            def pack(b, carry):
                pair_out[(p * n_chip + dest) * share + b] = summed(
                    0, (dest * CORES + other_core) * share + b)
                return carry

            lax.fori_loop(0, share, pack, 0)
            send(part(pair_out, dest), part(pair_in, dest), pair_send.at[p, d],
                 pair_recv.at[p, dest], partner)
        for d in order:
            dest = chip_peer[d]
            slot = part(pair_in, dest)
            remote(slot, slot, pair_send.at[p, d], pair_recv.at[p, dest], partner).wait_recv()

            def pack_push(b, carry):
                at = (p * n_chip + dest) * share + b
                value = summed(0, (dest * CORES + core) * share + b) + pair_in[at]
                if d == 0:
                    push_own[h * share + b] = value
                else:
                    push_out[at] = value.astype(bf16)
                return carry

            lax.fori_loop(0, share, pack_push, 0)
            if d != 0:
                send(part(push_out, dest), part(push_in, chip), push_send.at[p, d],
                     push_recv.at[p, chip], (i, dest * CORES + core))

    def update_dual(t, h):
        p = t * HALVES + h
        step = step_scale * weight[h]
        for d in range(1, n_chip):
            origin = chip_peer[n_chip - d]
            slot = push_in.at[pl.ds((p * n_chip + origin) * share, share)]
            remote(slot, slot, push_send.at[p, d], push_recv.at[p, origin],
                   (i, origin * CORES + core)).wait_recv()

        def one(b, carry):
            pushed = push_own[h * share + b]
            for d in range(1, n_chip):
                pushed = pushed + push_in[
                    (p * n_chip + chip_peer[d]) * share + b].astype(f32)
            change = step * (wanted[h * share + b] - pushed)
            new = dual[h * share + b] + change
            dual[h * share + b] = new
            if t < ITERS - 1:
                dual_rows[p + HALVES][j * share + b] = new.astype(bf16)
            return carry + squares(change)

        dual_sq = lax.fori_loop(0, share, one, zero)
        if t < ITERS - 1:
            gather_start(p + HALVES)
        norm_start(p + HALVES, dual_sq, primal_sq[h])

    for t in range(ITERS):
        for step in (pull, update_primal, push, update_dual):
            for h in range(HALVES):
                step(t, h)

    def together(ref, stride, b):
        return jnp.concatenate([ref[h * stride + b] for h in range(HALVES)], axis=0).T

    for h in range(HALVES):
        norm_middle(ITERS * HALVES + h)

    def finish_dual(b, carry):
        dual_out[b] = together(dual, share, b)
        return carry

    lax.fori_loop(0, share, finish_dual, 0)
    for d in range(n_row):
        origin = row_peer[n_row - d] if d else i
        if d:
            for h in range(HALVES):
                slot = final.at[pl.ds(h * blocks_c + origin * quarter, quarter)]
                remote(slot, slot, final_send.at[h, d], final_recv.at[h, origin],
                       (origin, j)).wait_recv()

        def finish_primal(b, carry):
            primal_out[origin * quarter + b] = together(final, blocks_c, origin * quarter + b)
            return carry

        lax.fori_loop(0, quarter, finish_primal, 0)
    for h in range(HALVES):
        new_weight(ITERS * HALVES + h, h)
    column = jnp.concatenate(weight, axis=0)
    weight_out[...] = jnp.broadcast_to(column, (width, width)).T[0:1, :]
    for copy in sends:
        copy.wait_send()


def on_device(
    tile_values, tile_rows, tile_cols, objective, demand, lower_bound, bound_span, bound_types,
    primal_start, dual_start,
):
    n_row, n_col = lax.axis_size("row"), lax.axis_size("col")
    total, size = tile_values.shape[0], tile_values.shape[1]
    width = demand.shape[1]
    share = dual_start.shape[0] // size
    blocks_r = share * n_col
    blocks_c = primal_start.shape[0] // size
    quarter = blocks_c // n_row
    n_chip = n_col // CORES
    keys = jnp.stack([tile_rows.reshape(-1), tile_cols.reshape(-1)])
    plan, ends = schedule(keys, keys[::-1], max(blocks_r, blocks_c))
    low = jnp.where(bound_types == 0, -jnp.inf, lower_bound)
    high = jnp.where(bound_types == 2, lower_bound + bound_span, jnp.inf)
    params = lax.dynamic_slice_in_dim(
        jnp.stack([objective, low, high]),
        lax.axis_index("row") * quarter * size, quarter * size, 1,
    )
    f32, bf16 = jnp.float32, jnp.bfloat16
    vmem, smem = pl.BlockSpec(memory_space=pltpu.VMEM), pl.BlockSpec(memory_space=pltpu.SMEM)
    anywhere = pl.BlockSpec(memory_space=pl.ANY)
    dma = pltpu.SemaphoreType.DMA
    phases = ITERS * HALVES
    norms = phases + HALVES

    def held(count, dtype):
        return pltpu.VMEM((count, width // HALVES, size), dtype)

    primal, dual, weight = pl.pallas_call(
        functools.partial(kernel, n_row, n_col),
        out_shape=(
            jax.ShapeDtypeStruct((blocks_c, size, width), f32),
            jax.ShapeDtypeStruct((share, size, width), f32),
            jax.ShapeDtypeStruct((1, width), f32),
        ),
        in_specs=[smem, smem, anywhere, vmem, vmem, anywhere, vmem],
        out_specs=(vmem, vmem, vmem),
        scratch_shapes=[
            pltpu.VMEM((total, size, size), bf16),
            pltpu.VMEM((quarter, size, width), f32),
            held(HALVES * quarter, f32),
            held(HALVES * share, f32),
            held(HALVES * share, f32),
            (held(blocks_r, bf16),) * phases,
            held(total, f32),
            held(phases * blocks_c, bf16),
            held(HALVES * quarter, f32),
            held(phases * blocks_c, bf16),
            (held(blocks_c, bf16),) * phases,
            held(phases * n_chip * share, f32),
            held(phases * n_chip * share, f32),
            held(phases * n_chip * share, bf16),
            held(HALVES * share, f32),
            held(phases * n_chip * share, bf16),
            held(HALVES * blocks_c, f32),
            pltpu.VMEM((norms * n_row, 8, width), f32),
            pltpu.VMEM((norms * n_col, 8, width), f32),
            dma((2,)),
            dma((phases, n_chip)), dma((phases, n_col)), dma((phases, n_chip)),
            dma((phases, n_row)), dma((phases, n_row)),
            dma((phases, n_row)), dma((phases, n_row)),
            dma((HALVES, n_row)), dma((HALVES, n_row)),
            dma((phases, n_chip)), dma((phases, n_chip)),
            dma((phases, n_chip)), dma((phases, n_chip)),
            dma((norms, n_row)), dma((norms, n_row)),
            dma((norms, n_col)), dma((norms, n_col)),
        ],
        compiler_params=pltpu.CompilerParams(
            collective_id=0, has_side_effects=True, vmem_limit_bytes=54 * 2**20
        ),
        cost_estimate=pl.CostEstimate(
            flops=4 * ITERS * total * size * size * width,
            bytes_accessed=2 * total * size * size, transcendentals=0,
        ),
    )(
        plan, ends, tile_values, params,
        demand.reshape(share, size, width),
        primal_start.reshape(blocks_c, size, width),
        dual_start.reshape(share, size, width),
    )
    return primal.reshape(primal_start.shape), dual.reshape(dual_start.shape), weight.reshape(width)


def solution(mesh):
    return jax.shard_map(
        on_device,
        mesh=mesh,
        in_specs=(
            P("row", "col", None),
            P("row", "col"),
            P("row", "col"),
            P("col"),
            P(("row", "col"), None),
            P("col"),
            P("col"),
            P("col"),
            P("col", None),
            P(("row", "col"), None),
        ),
        out_specs=(P("col", None), P(("row", "col"), None), P()),
        check_vma=False,
    )
```
